32 devices in a mesh: loop: 4 (over y, x), dp: 8 (over z, core).
Axes of the slice: x: 2, y: 2, z: 4, core: 2. Of those that a mesh axis runs over, the one named last changes fastest.
Arguments:
- tokens: bfloat16 [1792, 8192], P('dp', 'loop'), may hold values from -8 to 8
- weight: bfloat16 [8192, 14336], P('loop', 'dp'), as said below
- rounding: float32 [8192, 14336], P('loop', 'dp'), may hold values from -6 to 6
- floor_codes: int32 [8192, 14336], P('loop', 'dp'), may hold values from -1 to 15
- scale_codes: int32 [14336], P('dp'), may hold values from 12 to 15
- zero_codes: int32 [14336], P('dp'), may hold values from 0 to 15
- block_mask: int32 [128, 224], P('loop', 'dp'), may hold values from 0 to 1, as said below
Outputs:
- refined: float32 [8192, 14336], P('loop', 'dp')
The draws below stay inside these ranges and needn't reach their ends.
Inputs may be any that keep to these rules, and one draw needn't show every extreme that they name: weight equals scales times (floor_codes - zero_point + a fraction in [0, 1)), then is rounded to bfloat16. `block_mask`: the share of surviving blocks differs between column blocks.
All inputs are finite; a program needn't handle non-finite values.
Results may differ from the reference program's by a relative error of at most 0.019.
Values may be sent and summed in bfloat16 or wider, within the bound.
No kernel may reach another device: no remote copies, remote signals or barrier semaphores. Data moves between devices by JAX's collectives and lax.ppermute only.
A program may use at most 192 MiB of HBM per device.

```python
import jax
import jax.numpy as jnp
from jax import lax

D = 8192
FF = 14336
BLOCK = 64
ITERS = 2
TOKENS = 1792
N_LOOP = 4


def grid_codes(key):
    floor_codes = jax.random.randint(jax.random.fold_in(key, 11), (D, FF), -1, 16, dtype=jnp.int32)
    scale_codes = jax.random.randint(jax.random.fold_in(key, 12), (FF,), 12, 16, dtype=jnp.int32)
    zero_codes = jax.random.randint(jax.random.fold_in(key, 13), (FF,), 0, 16, dtype=jnp.int32)
    return (floor_codes, scale_codes, zero_codes)


def draw_floor_codes(key, part):
    return grid_codes(key)[0]


def draw_scale_codes(key, part):
    return grid_codes(key)[1]


def draw_zero_codes(key, part):
    return grid_codes(key)[2]


def draw_weight(key, part):
    floor_codes, scale_codes, zero_codes = grid_codes(key)
    scales = 0.02 * jnp.exp2(scale_codes.astype(jnp.float32) * 0.25)
    fraction = jax.random.uniform(jax.random.fold_in(key, 14), (D, FF), jnp.float32, 0.0, 1.0)
    values = scales[None, :] * (floor_codes.astype(jnp.float32) - zero_codes.astype(jnp.float32)[None, :] + fraction)
    return values.astype(jnp.bfloat16)


def draw_block_mask(key, part):
    density = jax.random.randint(jax.random.fold_in(key, 21), (FF // BLOCK,), 1, 8, dtype=jnp.int32)
    rolled = jax.random.randint(jax.random.fold_in(key, 22), (D // BLOCK, FF // BLOCK), 0, 8, dtype=jnp.int32)
    return (rolled < density[None, :]).astype(jnp.int32)


def block_scale(key, extent, split, least, high):
    def one(position, shards_of):
        heights = jax.random.uniform(jax.random.fold_in(jax.random.fold_in(key, 6), position), (shards_of,), jnp.float32, least / len(split), high / len(split))
        return jnp.repeat(jnp.exp(heights), extent[position] // shards_of).reshape((-1,) + (1,) * (len(extent) - position - 1))

    loudness = one(*split[0])
    for cut in split[1:]:
        loudness = loudness * one(*cut)
    return loudness


def centred(key, extent, deviation, limit, pieces=(), held_as=jnp.bfloat16):
    level = block_scale(key, extent, pieces, -0.22, 0.18) if pieces else 1.0
    entries = jax.random.normal(key, extent, jnp.float32) * deviation * level
    return jnp.minimum(jnp.maximum(entries, -limit), limit).astype(held_as)


def setup_inputs(seed: int = 0) -> dict:
    streams_of = jax.random.split(jax.random.key(seed), 8)
    tokens = centred(streams_of[0], (TOKENS, D), 2.0, 8.0, ((0, 8), (1, 4)))
    weight = draw_weight(jax.random.fold_in(streams_of[7], 71), 0)
    rounding = centred(streams_of[2], (D, FF), 1.0, 6.0, ((0, 4), (1, 8)), jnp.float32)
    floor_codes = draw_floor_codes(jax.random.fold_in(streams_of[7], 71), 0)
    scale_codes = draw_scale_codes(jax.random.fold_in(streams_of[7], 71), 0)
    zero_codes = draw_zero_codes(jax.random.fold_in(streams_of[7], 71), 0)
    block_mask = draw_block_mask(jax.random.fold_in(streams_of[7], 71), 0)
    return {"tokens": tokens, "weight": weight, "rounding": rounding, "floor_codes": floor_codes, "scale_codes": scale_codes, "zero_codes": zero_codes, "block_mask": block_mask}


step_rate = 20.0
reg_weight = 0.05
base_scale = 0.02


def expand(block_mask):
    row_blocks, col_blocks = block_mask.shape
    spread = jnp.broadcast_to(block_mask[:, None, :, None], (row_blocks, BLOCK, col_blocks, BLOCK))
    return spread.reshape(row_blocks * BLOCK, col_blocks * BLOCK).astype(jnp.float32)


def refine(tokens, weight, rounding, floor_codes, scales, zero_point, kept_mask):
    panel_width = weight.shape[1]
    floors = floor_codes.astype(jnp.float32)
    in_range = ((floor_codes >= 0) & (floor_codes <= 14)).astype(jnp.float32)
    target = weight.astype(jnp.float32)
    grouped = tokens.astype(jnp.float32).reshape(TOKENS, N_LOOP, D // N_LOOP)
    for iteration in range(ITERS):
        relaxed = jax.nn.sigmoid(rounding)
        levels = jnp.clip(floors + relaxed, 0.0, 15.0)
        w_delta = (kept_mask * (scales[None, :] * (levels - zero_point[None, :]) - target)).astype(jnp.bfloat16)
        delta_groups = w_delta.astype(jnp.float32).reshape(N_LOOP, D // N_LOOP, panel_width)
        partials = jnp.einsum("tkd,kdc->ktc", grouped, delta_groups, precision=lax.Precision.HIGHEST)
        rounded = lax.optimization_barrier(partials.astype(jnp.bfloat16))
        residual = jnp.sum(rounded.astype(jnp.float32), axis=0)
        scaled_err = ((2.0 / TOKENS) * residual).astype(jnp.bfloat16)
        gradient = jnp.dot(tokens.T, scaled_err, preferred_element_type=jnp.float32)
        centered = 2.0 * relaxed - 1.0
        descent = gradient * scales[None, :] * in_range - reg_weight * 8.0 * centered ** 3
        rounding = rounding - step_rate * kept_mask * descent * relaxed * (1.0 - relaxed)
    return rounding


def reference(tokens, weight, rounding, floor_codes, scale_codes, zero_codes, block_mask):
    panel_width = FF // 8
    scales_all = base_scale * jnp.exp2(scale_codes.astype(jnp.float32) * 0.25)
    zero_all = zero_codes.astype(jnp.float32)

    def one_panel(panel_index):
        first_col = (panel_index * panel_width).astype(jnp.int32)
        first_block = (panel_index * (panel_width // BLOCK)).astype(jnp.int32)
        weight_panel = lax.dynamic_slice_in_dim(weight, first_col, panel_width, 1)
        rounding_panel = lax.dynamic_slice_in_dim(rounding, first_col, panel_width, 1)
        floor_panel = lax.dynamic_slice_in_dim(floor_codes, first_col, panel_width, 1)
        scale_panel = lax.dynamic_slice_in_dim(scales_all, first_col, panel_width, 0)
        zero_panel = lax.dynamic_slice_in_dim(zero_all, first_col, panel_width, 0)
        mask_panel = lax.dynamic_slice_in_dim(block_mask, first_block, panel_width // BLOCK, 1)
        return refine(tokens, weight_panel, rounding_panel, floor_panel, scale_panel, zero_panel, expand(mask_panel))

    panels = lax.map(one_panel, jnp.arange(8, dtype=jnp.int32))
    return jnp.transpose(panels, (1, 0, 2)).reshape(D, FF)
```

```python
import jax
import jax.numpy as jnp
from jax import lax
from jax.experimental import pallas as pl
from jax.experimental.pallas import tpu as pltpu
from jax.sharding import PartitionSpec as P

BLOCK = 64
ITERS = 2
TILE = 256
STRIP = 16
ROWS = 512
VMEM_LIMIT = 24 * 1024 * 1024


step_rate = 20.0
reg_weight = 0.05
base_scale = 0.02

f32 = jnp.float32
bf16 = jnp.bfloat16


def expand(block_mask):
    row_blocks, col_blocks = block_mask.shape
    spread = jnp.broadcast_to(block_mask[:, None, :, None], (row_blocks, BLOCK, col_blocks, BLOCK))
    return spread.reshape(row_blocks * BLOCK, col_blocks * BLOCK).astype(jnp.float32)


def token_product(token_rows, scaled_err):
    return lax.dot_general(
        token_rows, scaled_err, (((0,), (0,)), ((), ())), preferred_element_type=jnp.float32
    )


def plain(tokens, weight, rounding, floor_codes, scale_codes, zero_codes, block_mask):
    gathered = lax.all_gather(tokens, "dp", axis=0, tiled=True)
    token_count = gathered.shape[0]
    scales = base_scale * jnp.exp2(scale_codes.astype(jnp.float32) * 0.25)
    zero_point = zero_codes.astype(jnp.float32)
    kept_mask = expand(block_mask)
    floors = floor_codes.astype(jnp.float32)
    in_range = ((floor_codes >= 0) & (floor_codes <= 14)).astype(jnp.float32)
    target = weight.astype(jnp.float32)
    for iteration in range(ITERS):
        relaxed = jax.nn.sigmoid(rounding)
        levels = jnp.clip(floors + relaxed, 0.0, 15.0)
        w_delta = (kept_mask * (scales[None, :] * (levels - zero_point[None, :]) - target)).astype(
            jnp.bfloat16
        )
        partial_sum = jnp.dot(gathered, w_delta, preferred_element_type=jnp.float32)
        residual = lax.psum(partial_sum.astype(jnp.bfloat16), "loop").astype(jnp.float32)
        scaled_err = (2.0 / token_count * residual).astype(jnp.bfloat16)
        gradient = token_product(gathered, scaled_err)
        centered = 2.0 * relaxed - 1.0
        descent = gradient * scales[None, :] * in_range - reg_weight * 8.0 * centered**3
        rounding = rounding - step_rate * kept_mask * descent * relaxed * (1.0 - relaxed)
    return rounding


KERNEL_FLOPS = 40_000_000_000
VMEM = pl.BlockSpec(memory_space=pltpu.VMEM)
ANY = pl.BlockSpec(memory_space=pl.ANY)
HBM = pl.BlockSpec(memory_space=pltpu.HBM)
SMEM = pl.BlockSpec(memory_space=pltpu.SMEM)


class Chain:
    def __init__(self):
        self.last = None

    def call(self, kernel, name, operands, in_specs, out_specs, out_shape, flops, moved, grid=(), scratch=(), aliases=None, late_hbm=False):
        count = len(operands)
        late = [] if self.last is None or late_hbm else [self.last]

        def wrapped(*refs):
            return kernel(*refs[:count], *refs[count + len(late):])

        out = pl.pallas_call(
            wrapped,
            grid=grid,
            in_specs=list(in_specs) + [ANY] * len(late),
            out_specs=out_specs,
            out_shape=out_shape,
            scratch_shapes=list(scratch),
            input_output_aliases=aliases or {},
            compiler_params=pltpu.CompilerParams(vmem_limit_bytes=VMEM_LIMIT),
            cost_estimate=pl.CostEstimate(flops=KERNEL_FLOPS, bytes_accessed=1024, transcendentals=0),
            name=name,
        )(*operands, *late)
        self.last = pltpu.with_memory_space_constraint(out[0], pltpu.HBM) if late_hbm else out[-1]
        return out


def delta_rows(half_tanh, floors, weight, scales, zeros, kept):
    levels = jnp.clip(floors + (0.5 + 0.5 * half_tanh), 0.0, 15.0)
    return (kept * (scales * (levels - zeros) - weight)).astype(bf16)


def update_rows(grad, t, v, code, scales, kept):
    square = t * t
    pull = jnp.where((code >= 0) & (code <= 14), grad * scales, 0.0)
    descent = pull - (8.0 * reg_weight) * (t * square)
    return v - ((0.25 * step_rate) * kept) * (1.0 - square) * descent


def by_rows(rows, body):
    def block(i, carry):
        for j in range(BLOCK // STRIP):
            body(pl.multiple_of(i * BLOCK + j * STRIP, STRIP), i)
        return carry

    lax.fori_loop(0, rows // BLOCK, block, 0)


def steps_of(codes):
    return base_scale * jnp.exp2(codes.astype(f32) * 0.25)


def first_delta(chain, col, cols, weight, rounding, floors, scale_codes, zeros, kept):
    d = weight.shape[0]
    wide = 512 if cols % 512 == 0 and col % 512 == 0 else TILE
    rows = min(d, 512 * 512 // wide)
    first = col // wide

    def kernel(s_ref, zp_ref, m, v, fl, w, out):
        def tile(v_t, fl_t, w_t):
            j, i = pl.program_id(0), pl.program_id(1)
            lanes = pl.ds(pl.multiple_of(j * wide, wide), wide)
            there = pl.ds(pl.multiple_of((first + j) * wide, wide), wide)
            s, zp = steps_of(s_ref[:, there]), zp_ref[:, there].astype(f32)

            def strip(start, b):
                at = pl.ds(start, STRIP)
                t = jnp.tanh(0.5 * v_t[at, :])
                mask = m[i * (rows // BLOCK) + b, :, there]
                out[pl.ds(pl.multiple_of(i * rows + start, STRIP), STRIP), lanes] = delta_rows(
                    t, fl_t[at, :].astype(f32), w_t[at, :].astype(f32), s, zp, mask)

            by_rows(rows, strip)

        spec = pl.BlockSpec((rows, wide), lambda j, i: (i, j + first))
        pltpu.emit_pipeline(tile, grid=(cols // wide, d // rows), in_specs=[spec] * 3)(v, fl, w)

    return chain.call(
        kernel, "delta", [scale_codes, zeros, kept, rounding, floors, weight],
        [VMEM] * 3 + [HBM] * 3, [VMEM], [jax.ShapeDtypeStruct((d, cols), bf16)], 20 * d * cols, 12 * d * cols,
    )[0]


def split_rows(part, bit, send, keep, at, cols):
    half = part.shape[0] // 2
    low, high = part[:half, :], part[half:, :]
    first = bit == 0
    keep[pl.ds(at, half), cols] = jnp.where(first, low, high).astype(bf16)
    send[pl.ds(at, half), cols] = jnp.where(first, high, low).astype(bf16)


def column_tiles(cols):
    return [(at, min(512, cols - at)) for at in range(0, cols, 512)]


def forward(chain, place, x, first, chunks, rows, deltas):
    d = x.shape[1]
    total = sum(a.shape[1] for a in deltas)

    def kernel(place_ref, x_ref, *refs):
        ws, (send, keep) = refs[:-2], refs[-2:]
        base = 0
        for w in ws:
            for at, cols in column_tiles(w.shape[1]):
                for i in range(chunks):
                    part = jnp.dot(x_ref[first + i * rows:first + (i + 1) * rows, :], w[:, at:at + cols], preferred_element_type=f32)
                    split_rows(part, place_ref[0], send, keep, i * (rows // 2), pl.ds(base + at, cols))
            base += w.shape[1]

    shape = jax.ShapeDtypeStruct((chunks * rows // 2, total), bf16)
    return chain.call(
        kernel, "forward", [place, x, *deltas], [SMEM] + [VMEM] * (1 + len(deltas)), [VMEM] * 2, [shape] * 2,
        2 * chunks * rows * d * total, 2 * d * (chunks * rows + total) // 4,
    )


def add(chain, a, b, scale=None):
    rows, cols = a.shape
    step = 32

    def kernel(a_ref, b_ref, out):
        def strip(i, carry):
            at = pl.ds(pl.multiple_of(i * step, step), step)
            total = a_ref[at, :].astype(f32) + b_ref[at, :].astype(f32)
            out[at, :] = (total if scale is None else scale * total).astype(bf16)
            return carry

        lax.fori_loop(0, rows // step, strip, 0)

    return chain.call(
        kernel, "pair" if scale is None else "err", [a, b], [VMEM] * 2, [VMEM],
        [jax.ShapeDtypeStruct(a.shape, bf16)], rows * cols, 6 * rows * cols,
    )[0]


def gate(chain, a):
    return chain.call(
        lambda a_ref, out: None, "gate", [a], [ANY], [ANY], [jax.ShapeDtypeStruct(a.shape, a.dtype)], 1, 1, aliases={0: 0}
    )[0]


def choose(chain, place, pieces, candidates, choices, name):
    arrays = pieces + candidates
    rows = [a.shape[0] for a in pieces] + [candidates[0].shape[0]] * len(choices) if candidates else [a.shape[0] for a in pieces]
    starts = [sum(rows[:i]) for i in range(len(rows))]
    width = arrays[0].shape[1]

    def kernel(place_ref, *refs):
        ins, (out, sems) = refs[:len(arrays)], refs[len(arrays):]

        def copy(ref, i):
            return pltpu.make_async_copy(ref, out.at[pl.ds(starts[i], rows[i]), :], sems.at[i])

        for i in range(len(pieces)):
            copy(ins[i], i).start()
        for z in range(4 if choices else 0):
            for core in range(2):
                @pl.when((place_ref[1] == z) & (place_ref[2] == core))
                def _(z=z, core=core):
                    picked = [copy(ins[len(pieces) + choice(z, core)], len(pieces) + i) for i, choice in enumerate(choices)]
                    for one in picked:
                        one.start()
                    for one in picked:
                        one.wait()
        for i in range(len(pieces)):
            copy(ins[i], i).wait()

    return chain.call(
        kernel, name, [place, *arrays], [SMEM] + [VMEM] * len(pieces) + [ANY] * len(candidates), [VMEM], [jax.ShapeDtypeStruct((sum(rows), width), bf16)],
        1, 4 * sum(rows) * width, scratch=[pltpu.SemaphoreType.DMA((len(rows),))],
    )[0]


def join(chain, place, mine, got, rows):
    half = rows // 2
    count = mine.shape[0] // half
    cols = mine.shape[1]

    def kernel(place_ref, mine_ref, got_ref, out):
        bit = place_ref[0]
        for i in range(count):
            def strip(k, carry):
                at = i * half + k * 32
                to = i * rows + k * 32
                out[pl.ds(pl.multiple_of(to + bit * half, 32), 32), :] = mine_ref[pl.ds(pl.multiple_of(at, 32), 32), :]
                out[pl.ds(pl.multiple_of(to + (1 - bit) * half, 32), 32), :] = got_ref[pl.ds(pl.multiple_of(at, 32), 32), :]
                return carry

            lax.fori_loop(0, half // 32, strip, 0)

    return chain.call(
        kernel, "join", [place, mine, got], [SMEM, VMEM, VMEM], [VMEM],
        [jax.ShapeDtypeStruct((count * rows, cols), bf16)], rows * cols, 6 * rows * cols,
    )[0]


def backward(chain, place, errs, starts, x_full, weight, rounding, v_col, floors, scales, zeros, kept, col, cols, out_prev, last):
    tokens, d = x_full.shape
    rows = tokens // 4
    n_err = len(errs)
    here = col // cols
    lanes = pl.ds(col, cols)

    def kernel(place_ref, *refs):
        e_refs, rest = refs[:n_err], list(refs[n_err:])
        x, s, zp, m, v, fl = rest[:6]
        rest = rest[6:]
        if last:
            if out_prev is not None:
                rest = rest[1:]
            out, err, grad = rest
            streams = [v, fl]
        else:
            w, out, send, keep, err, grad, delta = rest
            streams = [v, fl, w]
        if len(errs) == 1:
            (err,) = e_refs
        else:
            base = 0
            for ref, at in zip(e_refs, starts):
                err[base:base + ref.shape[0], :] = ref[:, at:at + cols]
                base += ref.shape[0]

        def tile(*tiles):
            v_t, fl_t, out_t = tiles[0], tiles[1], tiles[-1]
            g = pl.program_id(0)
            features = pl.ds(pl.multiple_of(g * ROWS, ROWS), ROWS)
            scales, zero = steps_of(s[:, lanes]), None if last else zp[:, lanes].astype(f32)
            grad[...] = lax.dot_general(x[:, features], err[...], (((0,), (0,)), ((), ())), preferred_element_type=f32)

            def strip(start, i):
                at = pl.ds(start, STRIP)
                code = fl_t[at, :]
                old = v_t[at, :]
                mask = m[g * (ROWS // BLOCK) + i, :, lanes]
                new = update_rows(grad[at, :], jnp.tanh(0.5 * old), old, code, scales, mask)
                out_t[at, :] = new
                if not last:
                    to = pl.ds(pl.multiple_of(g * ROWS + start, STRIP), STRIP)
                    delta[to, :] = delta_rows(jnp.tanh(0.5 * new), code.astype(f32), tiles[2][at, :].astype(f32), scales, zero, mask)

            by_rows(ROWS, strip)

        def spec(c):
            return pl.BlockSpec((ROWS, cols), lambda g: (g, c))

        pltpu.emit_pipeline(
            tile, grid=(d // ROWS,),
            in_specs=[spec(v_col // cols)] + [spec(here)] * (len(streams) - 1),
            out_specs=[spec(here if last else 0)],
        )(*streams, out)

        if not last:
            def two(c, carry):
                part = jnp.dot(x[pl.ds(pl.multiple_of(c * 2 * rows, 16), 2 * rows), :], delta[...], preferred_element_type=f32)
                at = pl.multiple_of(c * rows, 16)
                split_rows(part[:rows, :], place_ref[0], send, keep, at, slice(None))
                split_rows(part[rows:, :], place_ref[0], send, keep, at + rows // 2, slice(None))
                return carry

            lax.fori_loop(0, 2, two, 0)

    operands = [place, *errs, x_full, scales, zeros, kept, rounding, floors]
    in_specs = [SMEM] + [VMEM] * (n_err + 4) + [HBM] * 2
    scratch = [pltpu.VMEM((tokens, cols), bf16), pltpu.VMEM((ROWS, cols), f32)]
    aliases = {}
    if last:
        if out_prev is not None:
            aliases = {len(operands): 0}
            operands.append(out_prev)
            in_specs.append(HBM)
        out_specs = [HBM]
        out_shape = [pltpu.HBM(floors.shape, f32)]
    else:
        operands.append(weight)
        in_specs.append(HBM)
        out_specs = [HBM, VMEM, VMEM]
        out_shape = [pltpu.HBM((d, cols), f32)] + [jax.ShapeDtypeStruct((tokens // 2, cols), bf16)] * 2
        scratch.append(pltpu.VMEM((d, cols), bf16))
    return chain.call(
        kernel, "backward_last" if last else "backward_forward", operands, in_specs, out_specs, out_shape,
        (2 if last else 4) * tokens * d * cols, 16 * d * cols, scratch=scratch, aliases=aliases, late_hbm=last,
    )


def swap_loop(a, core0, core1, n):
    pairs = [(i * n + j, (i ^ (core1 if j % 2 else core0)) * n + j) for i in range(4) for j in range(n)]
    return lax.ppermute(a, ("loop", "dp"), pairs)


def swap_core(a, n):
    return lax.ppermute(a, "dp", [(i, i ^ 1) for i in range(n)])


def spread(a, step, n):
    pairs = []
    for z in range(n // 2):
        if z - step >= 0 and z + 1 < n // 2:
            pairs.append((2 * z, 2 * z + 2))
        if z + step < n // 2 and z - 1 >= 0:
            pairs.append((2 * z + 1, 2 * z - 1))
    return lax.ppermute(a, "dp", pairs)


ORDER = [
    "D0", "D1", "K0", "Fo0", "Fo1", "D2", "Po0", "Po1", "Fo2", "Eo0", "G1", "Eo1", "Po2", "Ro0", "K1", "Fn",
    "Ro1", "Eo2", "G2", "Pn", "Ro2", "K2", "Fm", "En", "G3", "Pm", "K3", "Ff0", "Rn", "Ff1", "Ff2", "Em",
    "Pf0", "Pf1", "Pf2", "Rm", "Ef0", "Ef1", "Ef2", "Rf0", "B0", "Rf1", "Rf2", "B1", "Ps0", "B2", "Ps1", "B3",
    "Es0", "Ps2", "Es1", "Ps3", "Rs0", "L0", "Es2", "Rs1", "L1", "Es3", "Rs2", "L2", "Rs3", "L3",
]


def piped(tokens, weight, rounding, floor_codes, scale_codes, zero_codes, block_mask):
    n = 8
    rows = 2 * tokens.shape[0]
    scale = 2.0 / (tokens.shape[0] * n)
    width = weight.shape[1]
    loop_at, dp_at = lax.axis_index("loop"), lax.axis_index("dp")
    core, z = dp_at % 2, dp_at // 2
    place = jnp.stack([jnp.where(core == 0, loop_at % 2, loop_at // 2), z, core]).astype(jnp.int32)
    scales, zeros = scale_codes[None, :], zero_codes[None, :]
    weight, rounding, floor_codes = (pltpu.with_memory_space_constraint(a, pltpu.HBM) for a in (weight, rounding, floor_codes))
    kept = jnp.repeat(block_mask.astype(f32), BLOCK, axis=1)[:, None, :]
    chain = Chain()

    blocks = [(0, 512), (512, 512), (1024, width - 1024)]
    groups = [(0, 512), (512, 512), (1024, 512), (1536, width - 1536)]
    other = swap_core(tokens, n)
    came, passed = {}, {}
    chunk, deltas, sent, kept_part, pairs, errs, second, out = {}, {}, {}, {}, {}, {}, {}, [None]

    def above(step):
        return lambda core: step - 1 if core == 1 else 3 + step - 1

    def below(step):
        return lambda core: step - 1 if core == 0 else 3 + step - 1

    near_of = [above(1), above(1), below(1), below(1)]
    mid_of = [above(2), below(1), above(1), below(2)]
    far_of = [above(3), above(2), below(2), below(3)]

    def home(col):
        i = max(i for i, (start, _) in enumerate(blocks) if start <= col)
        return i, col - blocks[i][0]

    for step in ORDER:
        kind, arg = step[0], step[1:]
        if kind == "K":
            if arg == "0":
                chunk["o"] = choose(chain, place, [tokens, other], [], [], "own")
                came[1] = spread(chunk["o"], 0, n)
            elif arg == "1":
                near = [lambda z, core: 0 if near_of[z](core) == 0 else 1]
                chunk["n"] = choose(chain, place, [], [came[1], passed[1]], near, "near")
            elif arg == "2":
                chunk["m"] = choose(chain, place, [], [came[1], came[2], passed[1], passed[2]],
                                    [lambda z, core: {0: 0, 1: 1, 3: 2, 4: 3}[mid_of[z](core)]], "mid")
            else:
                chunk["f"] = choose(chain, place, [chunk["o"], chunk["n"], chunk["m"]], [came[2], came[3], passed[2], passed[3]],
                                    [lambda z, core: {1: 0, 2: 1, 4: 2, 5: 3}[far_of[z](core)]], "all_tokens")
        elif kind == "G":
            i = int(arg)
            came[i] = gate(chain, came[i])
            passed[i] = swap_core(came[i], n)
            if i < 3:
                came[i + 1] = spread(came[i], i, n)
        elif kind == "D":
            i = int(arg)
            deltas[i] = first_delta(chain, *blocks[i], weight, rounding, floor_codes, scales, zeros, kept)
        elif kind == "F":
            ws = [deltas[int(arg[1])]] if len(arg) > 1 else [deltas[i] for i in range(len(blocks))]
            first, count = (3 * rows, 1) if arg[0] == "f" else (0, 1)
            sent[arg], kept_part[arg] = forward(chain, place, chunk[arg[0]], first, count, rows, ws)
        elif kind == "P":
            pairs[arg] = add(chain, kept_part[arg], swap_loop(sent[arg], 1, 2, n))
        elif kind == "E":
            mine = add(chain, pairs[arg], swap_loop(pairs[arg], 2, 1, n), scale)
            errs[arg] = (mine, swap_loop(mine, 1, 2, n))
        elif kind == "R":
            errs[arg] = join(chain, place, *errs[arg], rows)
        elif kind == "B":
            col, cols = groups[int(arg)]
            i, inner = home(col)
            second[arg], sent["s" + arg], kept_part["s" + arg] = backward(
                chain, place, [errs["o%d" % i], errs["n"], errs["m"], errs["f%d" % i]], [inner, col, col, inner],
                chunk["f"], weight, rounding, col, floor_codes, scales, zeros, kept, col, cols, None, False)
        elif kind == "L":
            col, cols = groups[int(arg)]
            (out[0],) = backward(
                chain, place, [errs["s" + arg]], [0],
                chunk["f"], weight, second[arg], 0, floor_codes, scales, zeros, kept, col, cols, out[0], True)
    return out[0]


def solution(mesh):
    placed = (
        P("dp", "loop"),
        P("loop", "dp"),
        P("loop", "dp"),
        P("loop", "dp"),
        P("dp"),
        P("dp"),
        P("loop", "dp"),
    )
    per_device = piped if (mesh.shape["loop"], mesh.shape["dp"]) == (4, 8) else plain
    return jax.shard_map(
        per_device, mesh=mesh, in_specs=placed, out_specs=P("loop", "dp"), check_vma=False
    )
```

```python
import jax
import jax.numpy as jnp
from jax import lax
from jax.experimental import pallas as pl
from jax.experimental.pallas import tpu as pltpu
from jax.sharding import PartitionSpec as P

BLOCK = 64
ITERS = 2
TILE = 256
STRIP = 16
ROWS = 512
MIB = 1024 * 1024


step_rate = 20.0
reg_weight = 0.05
base_scale = 0.02

f32 = jnp.float32
bf16 = jnp.bfloat16


def expand(block_mask):
    row_blocks, col_blocks = block_mask.shape
    spread = jnp.broadcast_to(block_mask[:, None, :, None], (row_blocks, BLOCK, col_blocks, BLOCK))
    return spread.reshape(row_blocks * BLOCK, col_blocks * BLOCK).astype(jnp.float32)


def token_product(token_rows, scaled_err):
    return lax.dot_general(
        token_rows, scaled_err, (((0,), (0,)), ((), ())), preferred_element_type=jnp.float32
    )


def plain(tokens, weight, rounding, floor_codes, scale_codes, zero_codes, block_mask):
    gathered = lax.all_gather(tokens, "dp", axis=0, tiled=True)
    token_count = gathered.shape[0]
    scales = base_scale * jnp.exp2(scale_codes.astype(jnp.float32) * 0.25)
    zero_point = zero_codes.astype(jnp.float32)
    kept_mask = expand(block_mask)
    floors = floor_codes.astype(jnp.float32)
    in_range = ((floor_codes >= 0) & (floor_codes <= 14)).astype(jnp.float32)
    target = weight.astype(jnp.float32)
    for iteration in range(ITERS):
        relaxed = jax.nn.sigmoid(rounding)
        levels = jnp.clip(floors + relaxed, 0.0, 15.0)
        w_delta = (kept_mask * (scales[None, :] * (levels - zero_point[None, :]) - target)).astype(
            jnp.bfloat16
        )
        partial_sum = jnp.dot(gathered, w_delta, preferred_element_type=jnp.float32)
        residual = lax.psum(partial_sum.astype(jnp.bfloat16), "loop").astype(jnp.float32)
        scaled_err = (2.0 / token_count * residual).astype(jnp.bfloat16)
        gradient = token_product(gathered, scaled_err)
        centered = 2.0 * relaxed - 1.0
        descent = gradient * scales[None, :] * in_range - reg_weight * 8.0 * centered**3
        rounding = rounding - step_rate * kept_mask * descent * relaxed * (1.0 - relaxed)
    return rounding


PEAK_PER_US = 1_000_000_000
VMEM = pl.BlockSpec(memory_space=pltpu.VMEM)
ANY = pl.BlockSpec(memory_space=pl.ANY)
HBM = pl.BlockSpec(memory_space=pltpu.HBM)
SMEM = pl.BlockSpec(memory_space=pltpu.SMEM)


class Chain:
    def __init__(self):
        self.last = None

    def call(self, kernel, name, operands, in_specs, out_specs, out_shape, us, grid=(), scratch=(), aliases=None, late_hbm=False, mib=6, late=-1):
        count = len(operands)
        before = [] if self.last is None or late_hbm else [self.last]

        def wrapped(*refs):
            return kernel(*refs[:count], *refs[count + len(before):])

        out = pl.pallas_call(
            wrapped,
            grid=grid,
            in_specs=list(in_specs) + [ANY] * len(before),
            out_specs=out_specs,
            out_shape=out_shape,
            scratch_shapes=list(scratch),
            input_output_aliases=aliases or {},
            compiler_params=pltpu.CompilerParams(vmem_limit_bytes=mib * MIB),
            cost_estimate=pl.CostEstimate(flops=int(us * PEAK_PER_US), bytes_accessed=1024, transcendentals=0),
            name=name,
        )(*operands, *before)
        self.last = pltpu.with_memory_space_constraint(out[0], pltpu.HBM) if late_hbm else out[late]
        return out


def delta_rows(half_tanh, floors, weight, scales, zeros, kept):
    levels = jnp.clip(floors + (0.5 + 0.5 * half_tanh), 0.0, 15.0)
    return (kept * (scales * (levels - zeros) - weight)).astype(bf16)


def update_rows(grad, t, v, code, scales, kept):
    square = t * t
    pull = jnp.where((code >= 0.0) & (code <= 14.0), grad * scales, 0.0)
    descent = pull - (8.0 * reg_weight) * (t * square)
    return v - ((0.25 * step_rate) * kept) * (1.0 - square) * descent


def by_rows(rows, body):
    def block(i, carry):
        for j in range(BLOCK // STRIP):
            body(pl.multiple_of(i * BLOCK + j * STRIP, STRIP), i)
        return carry

    lax.fori_loop(0, rows // BLOCK, block, 0, unroll=8)


def steps_of(codes):
    return base_scale * jnp.exp2(codes.astype(f32) * 0.25)


def first_delta(chain, col, cols, weight, rounding, floors, scale_codes, zeros, kept):
    d = weight.shape[0]
    rows = 512 if cols <= 512 else 256
    here = (slice(None), pl.ds(col, cols))

    def kernel(s_ref, zp_ref, m, v, fl, w, out, codes):
        def tile(v_t, fl_t, w_t, code_t):
            g = pl.program_id(0)
            for start, width in column_tiles(cols):
                lanes, there = pl.ds(start, width), pl.ds(col + start, width)
                s, zp = steps_of(s_ref[:, there]), zp_ref[:, there].astype(f32)

                def strip(first, b):
                    at = pl.ds(first, STRIP)
                    t = jnp.tanh(0.5 * v_t[at, lanes])
                    mask = m[g * (rows // BLOCK) + b, :, there]
                    code = fl_t[at, lanes].astype(f32)
                    code_t[at, lanes] = code.astype(bf16)
                    out[pl.ds(pl.multiple_of(g * rows + first, STRIP), STRIP), lanes] = delta_rows(
                        t, code, w_t[at, lanes].astype(f32), s, zp, mask)

                by_rows(rows, strip)

        spec = pl.BlockSpec((rows, cols), lambda g: (g, 0))
        pltpu.emit_pipeline(tile, grid=(d // rows,), in_specs=[spec] * 3, out_specs=[spec])(
            v.at[here], fl.at[here], w.at[here], codes)

    return chain.call(
        kernel, "delta", [scale_codes, zeros, kept, rounding, floors, weight],
        [VMEM] * 3 + [HBM] * 3, [VMEM, HBM], [jax.ShapeDtypeStruct((d, cols), bf16), pltpu.HBM((d, cols), bf16)],
        4.5 * cols / 512, mib=16, late=0,
    )


def split_rows(part, bit, send, keep, at, cols):
    half = part.shape[0] // 2
    low, high = part[:half, :], part[half:, :]
    first = bit == 0
    keep[pl.ds(at, half), cols] = jnp.where(first, low, high).astype(bf16)
    send[pl.ds(at, half), cols] = jnp.where(first, high, low).astype(bf16)


def column_tiles(cols):
    return [(at, min(512, cols - at)) for at in range(0, cols, 512)]


def forward(chain, place, x, first, rows, pieces):
    total = sum(cols for _, _, cols in pieces)

    def kernel(place_ref, x_ref, *refs):
        ws, (send, keep) = refs[:-2], refs[-2:]
        base = 0
        for w, (_, start, width) in zip(ws, pieces):
            for at, cols in column_tiles(width):
                part = jnp.dot(x_ref[first:first + rows, :], w[:, start + at:start + at + cols], preferred_element_type=f32)
                split_rows(part, place_ref[0], send, keep, 0, pl.ds(base + at, cols))
            base += width

    shape = jax.ShapeDtypeStruct((rows // 2, total), bf16)
    return chain.call(
        kernel, "forward", [place, x, *[w for w, _, _ in pieces]], [SMEM] + [VMEM] * (1 + len(pieces)), [VMEM] * 2, [shape] * 2,
        0.5 + 1.15 * total / 512, mib=16,
    )


def add(chain, a, b, scale=None):
    rows, cols = a.shape
    step = 32

    def kernel(a_ref, b_ref, out):
        def strip(i, carry):
            at = pl.ds(pl.multiple_of(i * step, step), step)
            total = a_ref[at, :].astype(f32) + b_ref[at, :].astype(f32)
            out[at, :] = (total if scale is None else scale * total).astype(bf16)
            return carry

        lax.fori_loop(0, rows // step, strip, 0)

    return chain.call(
        kernel, "pair" if scale is None else "err", [a, b], [VMEM] * 2, [VMEM],
        [jax.ShapeDtypeStruct(a.shape, bf16)], 0.4,
    )[0]


def gate(chain, a):
    return chain.call(
        lambda a_ref, out: None, "gate", [a], [ANY], [ANY], [jax.ShapeDtypeStruct(a.shape, a.dtype)], 0.1, aliases={0: 0}
    )[0]


def choose(chain, place, pieces, candidates, choices, name):
    arrays = pieces + candidates
    rows = [a.shape[0] for a in pieces] + [candidates[0].shape[0]] * len(choices) if candidates else [a.shape[0] for a in pieces]
    starts = [sum(rows[:i]) for i in range(len(rows))]
    width = arrays[0].shape[1]

    def kernel(place_ref, *refs):
        ins, (out, sems) = refs[:len(arrays)], refs[len(arrays):]

        def copy(ref, i):
            return pltpu.make_async_copy(ref, out.at[pl.ds(starts[i], rows[i]), :], sems.at[i])

        for i in range(len(pieces)):
            copy(ins[i], i).start()
        for z in range(4 if choices else 0):
            for core in range(2):
                @pl.when((place_ref[1] == z) & (place_ref[2] == core))
                def _(z=z, core=core):
                    picked = [copy(ins[len(pieces) + choice(z, core)], len(pieces) + i) for i, choice in enumerate(choices)]
                    for one in picked:
                        one.start()
                    for one in picked:
                        one.wait()
        for i in range(len(pieces)):
            copy(ins[i], i).wait()

    return chain.call(
        kernel, name, [place, *arrays], [SMEM] + [VMEM] * len(pieces) + [ANY] * len(candidates), [VMEM], [jax.ShapeDtypeStruct((sum(rows), width), bf16)],
        0.8, scratch=[pltpu.SemaphoreType.DMA((len(rows),))], mib=10,
    )[0]


def join(chain, place, mine, got, rows):
    half = rows // 2
    count = mine.shape[0] // half
    cols = mine.shape[1]

    def kernel(place_ref, mine_ref, got_ref, out):
        bit = place_ref[0]
        for i in range(count):
            def strip(k, carry):
                at = i * half + k * 32
                to = i * rows + k * 32
                out[pl.ds(pl.multiple_of(to + bit * half, 32), 32), :] = mine_ref[pl.ds(pl.multiple_of(at, 32), 32), :]
                out[pl.ds(pl.multiple_of(to + (1 - bit) * half, 32), 32), :] = got_ref[pl.ds(pl.multiple_of(at, 32), 32), :]
                return carry

            lax.fori_loop(0, half // 32, strip, 0)

    return chain.call(
        kernel, "join", [place, mine, got], [SMEM, VMEM, VMEM], [VMEM],
        [jax.ShapeDtypeStruct((count * rows, cols), bf16)], 0.6,
    )[0]


def backward(chain, place, errs, starts, x_full, weight, rounding, v_col, codes, code_col, scales, zeros, kept, col, cols, out_prev, last):
    tokens, d = x_full.shape
    rows = tokens // 4
    n_err = len(errs)
    here = col // cols
    lanes = pl.ds(col, cols)

    def kernel(place_ref, *refs):
        e_refs, rest = refs[:n_err], list(refs[n_err:])
        x, s, zp, m, v, fl = rest[:6]
        rest = rest[6:]
        if last:
            if out_prev is not None:
                rest = rest[1:]
            out, err, grad = rest
            streams = [v, fl]
        else:
            w, out, send, keep, err, grad, delta = rest
            streams = [v, fl, w]
        if len(errs) == 1:
            (err,) = e_refs
        else:
            base = 0
            for ref, at in zip(e_refs, starts):
                err[base:base + ref.shape[0], :] = ref[:, at:at + cols]
                base += ref.shape[0]

        def tile(*tiles):
            v_t, fl_t, out_t = tiles[0], tiles[1], tiles[-1]
            g = pl.program_id(0)
            features = pl.ds(pl.multiple_of(g * ROWS, ROWS), ROWS)
            scales, zero = steps_of(s[:, lanes]), None if last else zp[:, lanes].astype(f32)
            grad[...] = lax.dot_general(x[:, features], err[...], (((0,), (0,)), ((), ())), preferred_element_type=f32)

            def strip(start, i):
                at = pl.ds(start, STRIP)
                code = fl_t[at, :].astype(f32)
                old = v_t[at, :].astype(f32)
                mask = m[g * (ROWS // BLOCK) + i, :, lanes]
                new = update_rows(grad[at, :], jnp.tanh(0.5 * old), old, code, scales, mask)
                out_t[at, :] = new.astype(out_t.dtype)
                if not last:
                    to = pl.ds(pl.multiple_of(g * ROWS + start, STRIP), STRIP)
                    delta[to, :] = delta_rows(jnp.tanh(0.5 * new), code, tiles[2][at, :].astype(f32), scales, zero, mask)

            by_rows(ROWS, strip)

        def spec(c):
            return pl.BlockSpec((ROWS, cols), lambda g: (g, c))

        pltpu.emit_pipeline(
            tile, grid=(d // ROWS,),
            in_specs=[spec(v_col // cols), spec(code_col // cols)] + [spec(here)] * (len(streams) - 2),
            out_specs=[spec(here if last else 0)],
        )(*streams, out)

        if not last:
            def two(c, carry):
                part = jnp.dot(x[pl.ds(pl.multiple_of(c * 2 * rows, 16), 2 * rows), :], delta[...], preferred_element_type=f32)
                at = pl.multiple_of(c * rows, 16)
                split_rows(part[:rows, :], place_ref[0], send, keep, at, slice(None))
                split_rows(part[rows:, :], place_ref[0], send, keep, at + rows // 2, slice(None))
                return carry

            lax.fori_loop(0, 2, two, 0)

    operands = [place, *errs, x_full, scales, zeros, kept, rounding, codes]
    in_specs = [SMEM] + [VMEM] * (n_err + 4) + [HBM] * 2
    scratch = [pltpu.VMEM((tokens, cols), bf16), pltpu.VMEM((ROWS, cols), f32)]
    aliases = {}
    if last:
        if out_prev is not None:
            aliases = {len(operands): 0}
            operands.append(out_prev)
            in_specs.append(HBM)
        out_specs = [HBM]
        out_shape = [pltpu.HBM(weight.shape, f32)]
    else:
        operands.append(weight)
        in_specs.append(HBM)
        out_specs = [HBM, VMEM, VMEM]
        out_shape = [pltpu.HBM((d, cols), bf16)] + [jax.ShapeDtypeStruct((tokens // 2, cols), bf16)] * 2
        scratch.append(pltpu.VMEM((d, cols), bf16))
    return chain.call(
        kernel, "backward_last" if last else "backward_forward", operands, in_specs, out_specs, out_shape,
        (7.0 if last else 14.5) * cols / 512, scratch=scratch, aliases=aliases, late_hbm=last, mib=14 if last else 22,
    )


def swap_loop(a, core0, core1, n):
    pairs = [(i * n + j, (i ^ (core1 if j % 2 else core0)) * n + j) for i in range(4) for j in range(n)]
    return lax.ppermute(a, ("loop", "dp"), pairs)


def swap_core(a, n):
    return lax.ppermute(a, "dp", [(i, i ^ 1) for i in range(n)])


def spread(a, step, n):
    pairs = []
    for z in range(n // 2):
        if z - step >= 0 and z + 1 < n // 2:
            pairs.append((2 * z, 2 * z + 2))
        if z + step < n // 2 and z - 1 >= 0:
            pairs.append((2 * z + 1, 2 * z - 1))
    return lax.ppermute(a, "dp", pairs)


DELTAS = [512, 1280]
OWN = [512, 1280]
NEAR = [512, 1280]
MID = [512, 512, 768]
FAR = [512, 512, 768]
GROUPS = [512, 512, 512, 256]
ORDER = [
    "D0", "K0", "Fo0", "D1", "Po0", "Fo1", "Eo0", "G1", "Po1", "K1", "Fn0", "Fn1", "Ro0", "Eo1", "Pn0", "G2",
    "Pn1", "Ro1", "K2", "En0", "Fm0", "Fm1", "En1", "Fm2", "Rn0", "G3", "Pm0", "Pm1", "Rn1", "K3", "Ff0", "Pm2",
    "Em0", "Ff1", "Em1", "Pf0", "Ff2", "Em2", "Rm0", "Pf1", "Rm1", "Ef0", "Pf2", "Rm2", "Ef1", "Rf0", "B0", "Ef2",
    "Rf1", "B1", "Ps0", "Rf2", "B2", "Ps1", "B3", "Es0", "Ps2", "Es1", "Ps3", "Rs0", "L0", "Es2", "Rs1", "L1",
    "Es3", "Rs2", "L2", "Rs3", "L3",
]


def piped(tokens, weight, rounding, floor_codes, scale_codes, zero_codes, block_mask):
    n = 8
    rows = 2 * tokens.shape[0]
    scale = 2.0 / (tokens.shape[0] * n)
    width = weight.shape[1]
    loop_at, dp_at = lax.axis_index("loop"), lax.axis_index("dp")
    core, z = dp_at % 2, dp_at // 2
    place = jnp.stack([jnp.where(core == 0, loop_at % 2, loop_at // 2), z, core]).astype(jnp.int32)
    scales, zeros = scale_codes[None, :], zero_codes[None, :]
    weight, rounding, floor_codes = (pltpu.with_memory_space_constraint(a, pltpu.HBM) for a in (weight, rounding, floor_codes))
    kept = jnp.repeat(block_mask.astype(f32), BLOCK, axis=1)[:, None, :]
    chain = Chain()

    def ranges(widths):
        starts = [sum(widths[:i]) for i in range(len(widths))]
        return list(zip(starts, widths[:-1] + [width - starts[-1]]))

    blocks = ranges(DELTAS)
    parts = {"o": ranges(OWN), "n": ranges(NEAR), "m": ranges(MID), "f": ranges(FAR)}
    groups = ranges(GROUPS)
    other = swap_core(tokens, n)
    came, passed = {}, {}
    codes = {}
    chunk, deltas, sent, kept_part, pairs, errs, second, out = {}, {}, {}, {}, {}, {}, {}, [None]

    def above(step):
        return lambda core: step - 1 if core == 1 else 3 + step - 1

    def below(step):
        return lambda core: step - 1 if core == 0 else 3 + step - 1

    near_of = [above(1), above(1), below(1), below(1)]
    mid_of = [above(2), below(1), above(1), below(2)]
    far_of = [above(3), above(2), below(2), below(3)]

    def home(table, col):
        i = max(i for i, (start, _) in enumerate(table) if start <= col)
        return i, col - table[i][0]

    def pieces_of(col, cols):
        out = []
        for i, (start, count) in enumerate(blocks):
            low, high = max(start, col), min(start + count, col + cols)
            if low < high:
                out.append((deltas[i], low - start, high - low))
        return out

    for step in ORDER:
        kind, arg = step[0], step[1:]
        if kind == "K":
            if arg == "0":
                chunk["o"] = choose(chain, place, [tokens, other], [], [], "own")
                came[1] = spread(chunk["o"], 0, n)
            elif arg == "1":
                near = [lambda z, core: 0 if near_of[z](core) == 0 else 1]
                chunk["n"] = choose(chain, place, [], [came[1], passed[1]], near, "near")
            elif arg == "2":
                chunk["m"] = choose(chain, place, [], [came[1], came[2], passed[1], passed[2]],
                                    [lambda z, core: {0: 0, 1: 1, 3: 2, 4: 3}[mid_of[z](core)]], "mid")
            else:
                chunk["f"] = choose(chain, place, [chunk["o"], chunk["n"], chunk["m"]], [came[2], came[3], passed[2], passed[3]],
                                    [lambda z, core: {1: 0, 2: 1, 4: 2, 5: 3}[far_of[z](core)]], "all_tokens")
        elif kind == "G":
            i = int(arg)
            came[i] = gate(chain, came[i])
            passed[i] = swap_core(came[i], n)
            if i < 3:
                came[i + 1] = spread(came[i], i, n)
        elif kind == "D":
            i = int(arg)
            deltas[i], codes[i] = first_delta(chain, *blocks[i], weight, rounding, floor_codes, scales, zeros, kept)
        elif kind == "F":
            x, first = (chunk["f"], 3 * rows) if arg[0] == "f" else (chunk[arg[0]], 0)
            sent[arg], kept_part[arg] = forward(chain, place, x, first, rows, pieces_of(*parts[arg[0]][int(arg[1])]))
        elif kind == "P":
            pairs[arg] = add(chain, kept_part[arg], swap_loop(sent[arg], 1, 2, n))
        elif kind == "E":
            mine = add(chain, pairs[arg], swap_loop(pairs[arg], 2, 1, n), scale)
            errs[arg] = (mine, swap_loop(mine, 1, 2, n))
        elif kind == "R":
            errs[arg] = join(chain, place, *errs[arg], rows)
        elif kind == "B":
            col, cols = groups[int(arg)]
            i, inner = home(blocks, col)
            found = [(c, *home(parts[c], col)) for c in "onmf"]
            second[arg], sent["s" + arg], kept_part["s" + arg] = backward(
                chain, place, [errs["%s%d" % (c, k)] for c, k, _ in found], [at for _, _, at in found],
                chunk["f"], weight, rounding, col, codes[i], inner, scales, zeros, kept, col, cols, None, False)
        elif kind == "L":
            col, cols = groups[int(arg)]
            i, inner = home(blocks, col)
            (out[0],) = backward(
                chain, place, [errs["s" + arg]], [0],
                chunk["f"], weight, second[arg], 0, codes[i], inner, scales, zeros, kept, col, cols, out[0], True)
    return out[0]


def solution(mesh):
    placed = (
        P("dp", "loop"),
        P("loop", "dp"),
        P("loop", "dp"),
        P("loop", "dp"),
        P("dp"),
        P("dp"),
        P("loop", "dp"),
    )
    per_device = piped if (mesh.shape["loop"], mesh.shape["dp"]) == (4, 8) else plain
    return jax.shard_map(
        per_device, mesh=mesh, in_specs=placed, out_specs=P("loop", "dp"), check_vma=False
    )
```

```python
import jax
import jax.numpy as jnp
from jax import lax
from jax.experimental import pallas as pl
from jax.experimental.pallas import tpu as pltpu
from jax.sharding import PartitionSpec as P

BLOCK = 64
ITERS = 2
TILE = 256
STRIP = 16
ROWS = 512
MIB = 1024 * 1024


step_rate = 20.0
reg_weight = 0.05
base_scale = 0.02

f32 = jnp.float32
bf16 = jnp.bfloat16


def expand(block_mask):
    row_blocks, col_blocks = block_mask.shape
    spread = jnp.broadcast_to(block_mask[:, None, :, None], (row_blocks, BLOCK, col_blocks, BLOCK))
    return spread.reshape(row_blocks * BLOCK, col_blocks * BLOCK).astype(jnp.float32)


def token_product(token_rows, scaled_err):
    return lax.dot_general(
        token_rows, scaled_err, (((0,), (0,)), ((), ())), preferred_element_type=jnp.float32
    )


def plain(tokens, weight, rounding, floor_codes, scale_codes, zero_codes, block_mask):
    gathered = lax.all_gather(tokens, "dp", axis=0, tiled=True)
    token_count = gathered.shape[0]
    scales = base_scale * jnp.exp2(scale_codes.astype(jnp.float32) * 0.25)
    zero_point = zero_codes.astype(jnp.float32)
    kept_mask = expand(block_mask)
    floors = floor_codes.astype(jnp.float32)
    in_range = ((floor_codes >= 0) & (floor_codes <= 14)).astype(jnp.float32)
    target = weight.astype(jnp.float32)
    for iteration in range(ITERS):
        relaxed = jax.nn.sigmoid(rounding)
        levels = jnp.clip(floors + relaxed, 0.0, 15.0)
        w_delta = (kept_mask * (scales[None, :] * (levels - zero_point[None, :]) - target)).astype(
            jnp.bfloat16
        )
        partial_sum = jnp.dot(gathered, w_delta, preferred_element_type=jnp.float32)
        residual = lax.psum(partial_sum.astype(jnp.bfloat16), "loop").astype(jnp.float32)
        scaled_err = (2.0 / token_count * residual).astype(jnp.bfloat16)
        gradient = token_product(gathered, scaled_err)
        centered = 2.0 * relaxed - 1.0
        descent = gradient * scales[None, :] * in_range - reg_weight * 8.0 * centered**3
        rounding = rounding - step_rate * kept_mask * descent * relaxed * (1.0 - relaxed)
    return rounding


PEAK_PER_US = 1_000_000_000
VMEM = pl.BlockSpec(memory_space=pltpu.VMEM)
ANY = pl.BlockSpec(memory_space=pl.ANY)
HBM = pl.BlockSpec(memory_space=pltpu.HBM)
SMEM = pl.BlockSpec(memory_space=pltpu.SMEM)


class Chain:
    def __init__(self):
        self.last = None

    def call(self, kernel, name, operands, in_specs, out_specs, out_shape, us, grid=(), scratch=(), aliases=None, late_hbm=False, mib=6, late=-1):
        count = len(operands)
        before = [] if self.last is None or late_hbm else [self.last]

        def wrapped(*refs):
            return kernel(*refs[:count], *refs[count + len(before):])

        out = pl.pallas_call(
            wrapped,
            grid=grid,
            in_specs=list(in_specs) + [ANY] * len(before),
            out_specs=out_specs,
            out_shape=out_shape,
            scratch_shapes=list(scratch),
            input_output_aliases=aliases or {},
            compiler_params=pltpu.CompilerParams(vmem_limit_bytes=mib * MIB),
            cost_estimate=pl.CostEstimate(flops=int(us * PEAK_PER_US), bytes_accessed=1024, transcendentals=0),
            name=name,
        )(*operands, *before)
        self.last = pltpu.with_memory_space_constraint(out[0], pltpu.HBM) if late_hbm else out[late]
        return out


def delta_rows(half_tanh, floors, weight, scales, zeros, kept):
    levels = jnp.clip(floors + (0.5 + 0.5 * half_tanh), 0.0, 15.0)
    return (kept * (scales * (levels - zeros) - weight)).astype(bf16)


def update_rows(grad, t, v, code, scales, kept):
    square = t * t
    pull = jnp.where((code >= 0.0) & (code <= 14.0), grad * scales, 0.0)
    descent = pull - (8.0 * reg_weight) * (t * square)
    return v - ((0.25 * step_rate) * kept) * (1.0 - square) * descent


def by_rows(rows, body):
    def block(i, carry):
        for j in range(BLOCK // STRIP):
            body(pl.multiple_of(i * BLOCK + j * STRIP, STRIP), i)
        return carry

    lax.fori_loop(0, rows // BLOCK, block, 0, unroll=8)


def steps_of(codes):
    return base_scale * jnp.exp2(codes.astype(f32) * 0.25)


def first_delta(chain, col, cols, weight, rounding, floors, scale_codes, zeros, kept):
    d = weight.shape[0]
    rows = 512 if cols <= 512 else 256
    here = (slice(None), pl.ds(col, cols))

    def kernel(s_ref, zp_ref, m, v, fl, w, out, codes):
        def tile(v_t, fl_t, w_t, code_t):
            g = pl.program_id(0)
            for start, width in column_tiles(cols):
                lanes, there = pl.ds(start, width), pl.ds(col + start, width)
                s, zp = steps_of(s_ref[:, there]), zp_ref[:, there].astype(f32)

                def strip(first, b):
                    at = pl.ds(first, STRIP)
                    t = jnp.tanh(0.5 * v_t[at, lanes])
                    mask = m[g * (rows // BLOCK) + b, :, there]
                    code = fl_t[at, lanes].astype(f32)
                    code_t[at, lanes] = code.astype(bf16)
                    out[pl.ds(pl.multiple_of(g * rows + first, STRIP), STRIP), lanes] = delta_rows(
                        t, code, w_t[at, lanes].astype(f32), s, zp, mask)

                by_rows(rows, strip)

        spec = pl.BlockSpec((rows, cols), lambda g: (g, 0))
        pltpu.emit_pipeline(tile, grid=(d // rows,), in_specs=[spec] * 3, out_specs=[spec])(
            v.at[here], fl.at[here], w.at[here], codes)

    return chain.call(
        kernel, "delta", [scale_codes, zeros, kept, rounding, floors, weight],
        [VMEM] * 3 + [HBM] * 3, [VMEM, HBM], [jax.ShapeDtypeStruct((d, cols), bf16), pltpu.HBM((d, cols), bf16)],
        4.5 * cols / 512, mib=16, late=0,
    )


def split_rows(part, bit, send, keep, at, cols):
    half = part.shape[0] // 2
    low, high = part[:half, :], part[half:, :]
    first = bit == 0
    keep[pl.ds(at, half), cols] = jnp.where(first, low, high).astype(bf16)
    send[pl.ds(at, half), cols] = jnp.where(first, high, low).astype(bf16)


def column_tiles(cols):
    return [(at, min(512, cols - at)) for at in range(0, cols, 512)]


def forward(chain, place, x, first, rows, pieces):
    total = sum(cols for _, _, cols in pieces)

    def kernel(place_ref, x_ref, *refs):
        ws, (send, keep) = refs[:-2], refs[-2:]
        base = 0
        for w, (_, start, width) in zip(ws, pieces):
            for at, cols in column_tiles(width):
                part = jnp.dot(x_ref[first:first + rows, :], w[:, start + at:start + at + cols], preferred_element_type=f32)
                split_rows(part, place_ref[0], send, keep, 0, pl.ds(base + at, cols))
            base += width

    shape = jax.ShapeDtypeStruct((rows // 2, total), bf16)
    return chain.call(
        kernel, "forward", [place, x, *[w for w, _, _ in pieces]], [SMEM] + [VMEM] * (1 + len(pieces)), [VMEM] * 2, [shape] * 2,
        0.5 + 1.15 * total / 512, mib=16,
    )


def add(chain, a, b, scale=None):
    rows, cols = a.shape
    step = 32

    def kernel(a_ref, b_ref, out):
        def strip(i, carry):
            at = pl.ds(pl.multiple_of(i * step, step), step)
            total = a_ref[at, :].astype(f32) + b_ref[at, :].astype(f32)
            out[at, :] = (total if scale is None else scale * total).astype(bf16)
            return carry

        lax.fori_loop(0, rows // step, strip, 0)

    return chain.call(
        kernel, "pair" if scale is None else "err", [a, b], [VMEM] * 2, [VMEM],
        [jax.ShapeDtypeStruct(a.shape, bf16)], 0.4,
    )[0]


def gate(chain, a):
    return chain.call(
        lambda a_ref, out: None, "gate", [a], [ANY], [ANY], [jax.ShapeDtypeStruct(a.shape, a.dtype)], 0.1, aliases={0: 0}
    )[0]


def choose(chain, place, pieces, candidates, choices, name):
    arrays = pieces + candidates
    rows = [a.shape[0] for a in pieces] + [candidates[0].shape[0]] * len(choices) if candidates else [a.shape[0] for a in pieces]
    starts = [sum(rows[:i]) for i in range(len(rows))]
    width = arrays[0].shape[1]

    def kernel(place_ref, *refs):
        ins, (out, sems) = refs[:len(arrays)], refs[len(arrays):]

        def copy(ref, i):
            return pltpu.make_async_copy(ref, out.at[pl.ds(starts[i], rows[i]), :], sems.at[i])

        for i in range(len(pieces)):
            copy(ins[i], i).start()
        for z in range(4 if choices else 0):
            for core in range(2):
                @pl.when((place_ref[1] == z) & (place_ref[2] == core))
                def _(z=z, core=core):
                    picked = [copy(ins[len(pieces) + choice(z, core)], len(pieces) + i) for i, choice in enumerate(choices)]
                    for one in picked:
                        one.start()
                    for one in picked:
                        one.wait()
        for i in range(len(pieces)):
            copy(ins[i], i).wait()

    return chain.call(
        kernel, name, [place, *arrays], [SMEM] + [VMEM] * len(pieces) + [ANY] * len(candidates), [VMEM], [jax.ShapeDtypeStruct((sum(rows), width), bf16)],
        0.8, scratch=[pltpu.SemaphoreType.DMA((len(rows),))], mib=10,
    )[0]


def join(chain, place, mine, got, rows):
    half = rows // 2
    count = mine.shape[0] // half
    cols = mine.shape[1]

    def kernel(place_ref, mine_ref, got_ref, out):
        bit = place_ref[0]
        for i in range(count):
            def strip(k, carry):
                at = i * half + k * 32
                to = i * rows + k * 32
                out[pl.ds(pl.multiple_of(to + bit * half, 32), 32), :] = mine_ref[pl.ds(pl.multiple_of(at, 32), 32), :]
                out[pl.ds(pl.multiple_of(to + (1 - bit) * half, 32), 32), :] = got_ref[pl.ds(pl.multiple_of(at, 32), 32), :]
                return carry

            lax.fori_loop(0, half // 32, strip, 0)

    return chain.call(
        kernel, "join", [place, mine, got], [SMEM, VMEM, VMEM], [VMEM],
        [jax.ShapeDtypeStruct((count * rows, cols), bf16)], 0.6,
    )[0]


def backward(chain, place, errs, starts, x_full, weight, rounding, v_col, codes, code_col, scales, zeros, kept, col, cols, out_prev, last):
    tokens, d = x_full.shape
    rows = tokens // 4
    n_err = len(errs)
    here = col // cols
    lanes = pl.ds(col, cols)

    def kernel(place_ref, *refs):
        e_refs, rest = refs[:n_err], list(refs[n_err:])
        x, s, zp, m, v, fl = rest[:6]
        rest = rest[6:]
        if last:
            if out_prev is not None:
                rest = rest[1:]
            out, err, grad = rest
            streams = [v, fl]
        else:
            w, out, send, keep, err, grad, delta = rest
            streams = [v, fl, w]
        if len(errs) == 1:
            (err,) = e_refs
        else:
            base = 0
            for ref, at in zip(e_refs, starts):
                err[base:base + ref.shape[0], :] = ref[:, at:at + cols]
                base += ref.shape[0]

        def tile(*tiles):
            v_t, fl_t, out_t = tiles[0], tiles[1], tiles[-1]
            g = pl.program_id(0)
            features = pl.ds(pl.multiple_of(g * ROWS, ROWS), ROWS)
            scales, zero = steps_of(s[:, lanes]), None if last else zp[:, lanes].astype(f32)
            grad[...] = lax.dot_general(x[:, features], err[...], (((0,), (0,)), ((), ())), preferred_element_type=f32)

            def strip(start, i):
                at = pl.ds(start, STRIP)
                code = fl_t[at, :].astype(f32)
                old = v_t[at, :].astype(f32)
                mask = m[g * (ROWS // BLOCK) + i, :, lanes]
                new = update_rows(grad[at, :], jnp.tanh(0.5 * old), old, code, scales, mask)
                out_t[at, :] = new.astype(out_t.dtype)
                if not last:
                    to = pl.ds(pl.multiple_of(g * ROWS + start, STRIP), STRIP)
                    delta[to, :] = delta_rows(jnp.tanh(0.5 * new), code, tiles[2][at, :].astype(f32), scales, zero, mask)

            by_rows(ROWS, strip)

        def spec(c):
            return pl.BlockSpec((ROWS, cols), lambda g: (g, c))

        pltpu.emit_pipeline(
            tile, grid=(d // ROWS,),
            in_specs=[spec(v_col // cols), spec(code_col // cols)] + [spec(here)] * (len(streams) - 2),
            out_specs=[spec(here if last else 0)],
        )(*streams, out)

        if not last:
            def two(c, carry):
                part = jnp.dot(x[pl.ds(pl.multiple_of(c * 2 * rows, 16), 2 * rows), :], delta[...], preferred_element_type=f32)
                at = pl.multiple_of(c * rows, 16)
                split_rows(part[:rows, :], place_ref[0], send, keep, at, slice(None))
                split_rows(part[rows:, :], place_ref[0], send, keep, at + rows // 2, slice(None))
                return carry

            lax.fori_loop(0, 2, two, 0)

    operands = [place, *errs, x_full, scales, zeros, kept, rounding, codes]
    in_specs = [SMEM] + [VMEM] * (n_err + 4) + [HBM] * 2
    scratch = [pltpu.VMEM((tokens, cols), bf16), pltpu.VMEM((ROWS, cols), f32)]
    aliases = {}
    if last:
        if out_prev is not None:
            aliases = {len(operands): 0}
            operands.append(out_prev)
            in_specs.append(HBM)
        out_specs = [HBM]
        out_shape = [pltpu.HBM(weight.shape, f32)]
    else:
        operands.append(weight)
        in_specs.append(HBM)
        out_specs = [HBM, VMEM, VMEM]
        out_shape = [pltpu.HBM((d, cols), bf16)] + [jax.ShapeDtypeStruct((tokens // 2, cols), bf16)] * 2
        scratch.append(pltpu.VMEM((d, cols), bf16))
    return chain.call(
        kernel, "backward_last" if last else "backward_forward", operands, in_specs, out_specs, out_shape,
        (7.0 if last else 14.5) * cols / 512, scratch=scratch, aliases=aliases, late_hbm=last, mib=14 if last else 22,
    )


def swap_loop(a, core0, core1, n):
    pairs = [(i * n + j, (i ^ (core1 if j % 2 else core0)) * n + j) for i in range(4) for j in range(n)]
    return lax.ppermute(a, ("loop", "dp"), pairs)


def swap_core(a, n):
    return lax.ppermute(a, "dp", [(i, i ^ 1) for i in range(n)])


def spread(a, step, n):
    pairs = []
    for z in range(n // 2):
        if z - step >= 0 and z + 1 < n // 2:
            pairs.append((2 * z, 2 * z + 2))
        if z + step < n // 2 and z - 1 >= 0:
            pairs.append((2 * z + 1, 2 * z - 1))
    return lax.ppermute(a, "dp", pairs)


DELTAS = [512, 1280]
OWN = [512, 1280]
NEAR = [512, 1280]
MID = [512, 512, 768]
FAR = [512, 512, 768]
GROUPS = [512, 512, 512, 256]
ORDER = [
    "D0", "K0", "Fo0", "D1", "Po0", "Fo1", "Eo0", "G1", "K1", "Po1", "Fn0", "Fn1", "Ro0", "Eo1", "Pn0", "G2",
    "K2", "Pn1", "Fm0", "Ro1", "En0", "Fm1", "En1", "G3", "Fm2", "Rn0", "K3", "Ff0", "Pm0", "Pm1", "Ff1", "Pf0",
    "Rn1", "Em0", "Pf1", "Ff2", "Ef0", "Em1", "Ef1", "Pm2", "Rm0", "Pf2", "Rf0", "B0", "Em2", "Rf1", "Rm1", "Ef2",
    "B1", "Ps0", "Rm2", "Rf2", "B2", "Ps1", "Es0", "B3", "Ps2", "Es1", "Ps3", "Rs0", "L0", "Es2", "Rs1", "L1",
    "Es3", "Rs2", "L2", "Rs3", "L3",
]


def piped(tokens, weight, rounding, floor_codes, scale_codes, zero_codes, block_mask):
    n = 8
    rows = 2 * tokens.shape[0]
    scale = 2.0 / (tokens.shape[0] * n)
    width = weight.shape[1]
    loop_at, dp_at = lax.axis_index("loop"), lax.axis_index("dp")
    core, z = dp_at % 2, dp_at // 2
    place = jnp.stack([jnp.where(core == 0, loop_at % 2, loop_at // 2), z, core]).astype(jnp.int32)
    scales, zeros = scale_codes[None, :], zero_codes[None, :]
    weight, rounding, floor_codes = (pltpu.with_memory_space_constraint(a, pltpu.HBM) for a in (weight, rounding, floor_codes))
    kept = jnp.repeat(block_mask.astype(f32), BLOCK, axis=1)[:, None, :]
    chain = Chain()

    def ranges(widths):
        starts = [sum(widths[:i]) for i in range(len(widths))]
        return list(zip(starts, widths[:-1] + [width - starts[-1]]))

    blocks = ranges(DELTAS)
    parts = {"o": ranges(OWN), "n": ranges(NEAR), "m": ranges(MID), "f": ranges(FAR)}
    groups = ranges(GROUPS)
    other = swap_core(tokens, n)
    came, passed = {}, {}
    codes = {}
    chunk, deltas, sent, kept_part, pairs, errs, second, out = {}, {}, {}, {}, {}, {}, {}, [None]

    def above(step):
        return lambda core: step - 1 if core == 1 else 3 + step - 1

    def below(step):
        return lambda core: step - 1 if core == 0 else 3 + step - 1

    near_of = [above(1), above(1), below(1), below(1)]
    mid_of = [above(2), below(1), above(1), below(2)]
    far_of = [above(3), above(2), below(2), below(3)]

    def home(table, col):
        i = max(i for i, (start, _) in enumerate(table) if start <= col)
        return i, col - table[i][0]

    def pieces_of(col, cols):
        out = []
        for i, (start, count) in enumerate(blocks):
            low, high = max(start, col), min(start + count, col + cols)
            if low < high:
                out.append((deltas[i], low - start, high - low))
        return out

    for step in ORDER:
        kind, arg = step[0], step[1:]
        if kind == "K":
            if arg == "0":
                chunk["o"] = choose(chain, place, [tokens, other], [], [], "own")
                came[1] = spread(chunk["o"], 0, n)
            elif arg == "1":
                near = [lambda z, core: 0 if near_of[z](core) == 0 else 1]
                chunk["n"] = choose(chain, place, [], [came[1], passed[1]], near, "near")
            elif arg == "2":
                chunk["m"] = choose(chain, place, [], [came[1], came[2], passed[1], passed[2]],
                                    [lambda z, core: {0: 0, 1: 1, 3: 2, 4: 3}[mid_of[z](core)]], "mid")
            else:
                chunk["f"] = choose(chain, place, [chunk["o"], chunk["n"], chunk["m"]], [came[2], came[3], passed[2], passed[3]],
                                    [lambda z, core: {1: 0, 2: 1, 4: 2, 5: 3}[far_of[z](core)]], "all_tokens")
        elif kind == "G":
            i = int(arg)
            came[i] = gate(chain, came[i])
            passed[i] = swap_core(came[i], n)
            if i < 3:
                came[i + 1] = spread(came[i], i, n)
        elif kind == "D":
            i = int(arg)
            deltas[i], codes[i] = first_delta(chain, *blocks[i], weight, rounding, floor_codes, scales, zeros, kept)
        elif kind == "F":
            x, first = (chunk["f"], 3 * rows) if arg[0] == "f" else (chunk[arg[0]], 0)
            sent[arg], kept_part[arg] = forward(chain, place, x, first, rows, pieces_of(*parts[arg[0]][int(arg[1])]))
        elif kind == "P":
            pairs[arg] = add(chain, kept_part[arg], swap_loop(sent[arg], 1, 2, n))
        elif kind == "E":
            mine = add(chain, pairs[arg], swap_loop(pairs[arg], 2, 1, n), scale)
            errs[arg] = (mine, swap_loop(mine, 1, 2, n))
        elif kind == "R":
            errs[arg] = join(chain, place, *errs[arg], rows)
        elif kind == "B":
            col, cols = groups[int(arg)]
            i, inner = home(blocks, col)
            found = [(c, *home(parts[c], col)) for c in "onmf"]
            second[arg], sent["s" + arg], kept_part["s" + arg] = backward(
                chain, place, [errs["%s%d" % (c, k)] for c, k, _ in found], [at for _, _, at in found],
                chunk["f"], weight, rounding, col, codes[i], inner, scales, zeros, kept, col, cols, None, False)
        elif kind == "L":
            col, cols = groups[int(arg)]
            i, inner = home(blocks, col)
            (out[0],) = backward(
                chain, place, [errs["s" + arg]], [0],
                chunk["f"], weight, second[arg], 0, codes[i], inner, scales, zeros, kept, col, cols, out[0], True)
    return out[0]


def solution(mesh):
    placed = (
        P("dp", "loop"),
        P("loop", "dp"),
        P("loop", "dp"),
        P("loop", "dp"),
        P("dp"),
        P("dp"),
        P("loop", "dp"),
    )
    per_device = piped if (mesh.shape["loop"], mesh.shape["dp"]) == (4, 8) else plain
    return jax.shard_map(
        per_device, mesh=mesh, in_specs=placed, out_specs=P("loop", "dp"), check_vma=False
    )
```

```python
import jax
import jax.numpy as jnp
from jax import lax
from jax.experimental import pallas as pl
from jax.experimental.pallas import tpu as pltpu
from jax.sharding import PartitionSpec as P

BLOCK = 64
ITERS = 2
TILE = 256
STRIP = 16
ROWS = 512
MIB = 1024 * 1024


step_rate = 20.0
reg_weight = 0.05
base_scale = 0.02

f32 = jnp.float32
bf16 = jnp.bfloat16


def expand(block_mask):
    row_blocks, col_blocks = block_mask.shape
    spread = jnp.broadcast_to(block_mask[:, None, :, None], (row_blocks, BLOCK, col_blocks, BLOCK))
    return spread.reshape(row_blocks * BLOCK, col_blocks * BLOCK).astype(jnp.float32)


def token_product(token_rows, scaled_err):
    return lax.dot_general(
        token_rows, scaled_err, (((0,), (0,)), ((), ())), preferred_element_type=jnp.float32
    )


def plain(tokens, weight, rounding, floor_codes, scale_codes, zero_codes, block_mask):
    gathered = lax.all_gather(tokens, "dp", axis=0, tiled=True)
    token_count = gathered.shape[0]
    scales = base_scale * jnp.exp2(scale_codes.astype(jnp.float32) * 0.25)
    zero_point = zero_codes.astype(jnp.float32)
    kept_mask = expand(block_mask)
    floors = floor_codes.astype(jnp.float32)
    in_range = ((floor_codes >= 0) & (floor_codes <= 14)).astype(jnp.float32)
    target = weight.astype(jnp.float32)
    for iteration in range(ITERS):
        relaxed = jax.nn.sigmoid(rounding)
        levels = jnp.clip(floors + relaxed, 0.0, 15.0)
        w_delta = (kept_mask * (scales[None, :] * (levels - zero_point[None, :]) - target)).astype(
            jnp.bfloat16
        )
        partial_sum = jnp.dot(gathered, w_delta, preferred_element_type=jnp.float32)
        residual = lax.psum(partial_sum.astype(jnp.bfloat16), "loop").astype(jnp.float32)
        scaled_err = (2.0 / token_count * residual).astype(jnp.bfloat16)
        gradient = token_product(gathered, scaled_err)
        centered = 2.0 * relaxed - 1.0
        descent = gradient * scales[None, :] * in_range - reg_weight * 8.0 * centered**3
        rounding = rounding - step_rate * kept_mask * descent * relaxed * (1.0 - relaxed)
    return rounding


PEAK_PER_US = 1_000_000_000
VMEM = pl.BlockSpec(memory_space=pltpu.VMEM)
ANY = pl.BlockSpec(memory_space=pl.ANY)
HBM = pl.BlockSpec(memory_space=pltpu.HBM)
SMEM = pl.BlockSpec(memory_space=pltpu.SMEM)


class Chain:
    def __init__(self):
        self.last = None

    def call(self, kernel, name, operands, in_specs, out_specs, out_shape, us, grid=(), scratch=(), aliases=None, late_hbm=False, mib=6, late=-1):
        count = len(operands)
        before = [] if self.last is None or late_hbm else [self.last]

        def wrapped(*refs):
            return kernel(*refs[:count], *refs[count + len(before):])

        out = pl.pallas_call(
            wrapped,
            grid=grid,
            in_specs=list(in_specs) + [ANY] * len(before),
            out_specs=out_specs,
            out_shape=out_shape,
            scratch_shapes=list(scratch),
            input_output_aliases=aliases or {},
            compiler_params=pltpu.CompilerParams(vmem_limit_bytes=mib * MIB),
            cost_estimate=pl.CostEstimate(flops=int(us * PEAK_PER_US), bytes_accessed=1024, transcendentals=0),
            name=name,
        )(*operands, *before)
        self.last = pltpu.with_memory_space_constraint(out[0], pltpu.HBM) if late_hbm else out[late]
        return out


def delta_rows(half_tanh, floors, weight, scales, zeros, kept):
    levels = jnp.clip(floors + (0.5 + 0.5 * half_tanh), 0.0, 15.0)
    return (kept * (scales * (levels - zeros) - weight)).astype(bf16)


def update_rows(grad, t, v, code, scales, kept):
    square = t * t
    pull = jnp.where((code >= 0.0) & (code <= 14.0), grad * scales, 0.0)
    descent = pull - (8.0 * reg_weight) * (t * square)
    return v - ((0.25 * step_rate) * kept) * (1.0 - square) * descent


def by_rows(rows, body):
    def block(i, carry):
        for j in range(BLOCK // STRIP):
            body(pl.multiple_of(i * BLOCK + j * STRIP, STRIP), i)
        return carry

    lax.fori_loop(0, rows // BLOCK, block, 0, unroll=8)


def steps_of(codes):
    return base_scale * jnp.exp2(codes.astype(f32) * 0.25)


def first_delta(chain, col, cols, weight, rounding, floors, scale_codes, zeros, kept):
    d = weight.shape[0]
    rows = 512 if cols <= 512 else 256
    here = (slice(None), pl.ds(col, cols))

    def kernel(s_ref, zp_ref, m, v, fl, w, out, codes):
        def tile(v_t, fl_t, w_t, code_t):
            g = pl.program_id(0)
            for start, width in column_tiles(cols):
                lanes, there = pl.ds(start, width), pl.ds(col + start, width)
                s, zp = steps_of(s_ref[:, there]), zp_ref[:, there].astype(f32)

                def strip(first, b):
                    at = pl.ds(first, STRIP)
                    t = jnp.tanh(0.5 * v_t[at, lanes])
                    mask = m[g * (rows // BLOCK) + b, :, there]
                    code = fl_t[at, lanes].astype(f32)
                    code_t[at, lanes] = code.astype(bf16)
                    out[pl.ds(pl.multiple_of(g * rows + first, STRIP), STRIP), lanes] = delta_rows(
                        t, code, w_t[at, lanes].astype(f32), s, zp, mask)

                by_rows(rows, strip)

        spec = pl.BlockSpec((rows, cols), lambda g: (g, 0))
        pltpu.emit_pipeline(tile, grid=(d // rows,), in_specs=[spec] * 3, out_specs=[spec])(
            v.at[here], fl.at[here], w.at[here], codes)

    return chain.call(
        kernel, "delta", [scale_codes, zeros, kept, rounding, floors, weight],
        [VMEM] * 3 + [HBM] * 3, [VMEM, HBM], [jax.ShapeDtypeStruct((d, cols), bf16), pltpu.HBM((d, cols), bf16)],
        4.5 * cols / 512, mib=16, late=0,
    )


def split_rows(part, bit, send, keep, at, cols):
    half = part.shape[0] // 2
    low, high = part[:half, :], part[half:, :]
    first = bit == 0
    keep[pl.ds(at, half), cols] = jnp.where(first, low, high).astype(bf16)
    send[pl.ds(at, half), cols] = jnp.where(first, high, low).astype(bf16)


def column_tiles(cols):
    return [(at, min(512, cols - at)) for at in range(0, cols, 512)]


def forward(chain, place, x, first, rows, pieces):
    total = sum(cols for _, _, cols in pieces)

    def kernel(place_ref, x_ref, *refs):
        ws, (send, keep) = refs[:-2], refs[-2:]
        base = 0
        for w, (_, start, width) in zip(ws, pieces):
            for at, cols in column_tiles(width):
                part = jnp.dot(x_ref[first:first + rows, :], w[:, start + at:start + at + cols], preferred_element_type=f32)
                split_rows(part, place_ref[0], send, keep, 0, pl.ds(base + at, cols))
            base += width

    shape = jax.ShapeDtypeStruct((rows // 2, total), bf16)
    return chain.call(
        kernel, "forward", [place, x, *[w for w, _, _ in pieces]], [SMEM] + [VMEM] * (1 + len(pieces)), [VMEM] * 2, [shape] * 2,
        0.5 + 1.15 * total / 512, mib=16,
    )


def add(chain, a, b, scale=None):
    rows, cols = a.shape
    step = 32

    def kernel(a_ref, b_ref, out):
        def strip(i, carry):
            at = pl.ds(pl.multiple_of(i * step, step), step)
            total = a_ref[at, :].astype(f32) + b_ref[at, :].astype(f32)
            out[at, :] = (total if scale is None else scale * total).astype(bf16)
            return carry

        lax.fori_loop(0, rows // step, strip, 0)

    return chain.call(
        kernel, "pair" if scale is None else "err", [a, b], [VMEM] * 2, [VMEM],
        [jax.ShapeDtypeStruct(a.shape, bf16)], 0.4,
    )[0]


def gate(chain, a):
    return chain.call(
        lambda a_ref, out: None, "gate", [a], [ANY], [ANY], [jax.ShapeDtypeStruct(a.shape, a.dtype)], 0.1, aliases={0: 0}
    )[0]


def choose(chain, place, pieces, candidates, choices, name):
    arrays = pieces + candidates
    rows = [a.shape[0] for a in pieces] + [candidates[0].shape[0]] * len(choices) if candidates else [a.shape[0] for a in pieces]
    starts = [sum(rows[:i]) for i in range(len(rows))]
    width = arrays[0].shape[1]

    def kernel(place_ref, *refs):
        ins, (out, sems) = refs[:len(arrays)], refs[len(arrays):]

        def copy(ref, i):
            return pltpu.make_async_copy(ref, out.at[pl.ds(starts[i], rows[i]), :], sems.at[i])

        for i in range(len(pieces)):
            copy(ins[i], i).start()
        for z in range(4 if choices else 0):
            for core in range(2):
                @pl.when((place_ref[1] == z) & (place_ref[2] == core))
                def _(z=z, core=core):
                    picked = [copy(ins[len(pieces) + choice(z, core)], len(pieces) + i) for i, choice in enumerate(choices)]
                    for one in picked:
                        one.start()
                    for one in picked:
                        one.wait()
        for i in range(len(pieces)):
            copy(ins[i], i).wait()

    return chain.call(
        kernel, name, [place, *arrays], [SMEM] + [VMEM] * len(pieces) + [ANY] * len(candidates), [VMEM], [jax.ShapeDtypeStruct((sum(rows), width), bf16)],
        0.8, scratch=[pltpu.SemaphoreType.DMA((len(rows),))], mib=10,
    )[0]


def join(chain, place, mine, got, rows):
    half = rows // 2
    count = mine.shape[0] // half
    cols = mine.shape[1]

    def kernel(place_ref, mine_ref, got_ref, out):
        bit = place_ref[0]
        for i in range(count):
            def strip(k, carry):
                at = i * half + k * 32
                to = i * rows + k * 32
                out[pl.ds(pl.multiple_of(to + bit * half, 32), 32), :] = mine_ref[pl.ds(pl.multiple_of(at, 32), 32), :]
                out[pl.ds(pl.multiple_of(to + (1 - bit) * half, 32), 32), :] = got_ref[pl.ds(pl.multiple_of(at, 32), 32), :]
                return carry

            lax.fori_loop(0, half // 32, strip, 0)

    return chain.call(
        kernel, "join", [place, mine, got], [SMEM, VMEM, VMEM], [VMEM],
        [jax.ShapeDtypeStruct((count * rows, cols), bf16)], 0.6,
    )[0]


def backward(chain, place, errs, starts, x_full, weight, rounding, v_col, codes, code_col, scales, zeros, kept, col, cols, out_prev, last):
    tokens, d = x_full.shape
    rows = tokens // 4
    n_err = len(errs)
    here = col // cols
    lanes = pl.ds(col, cols)

    def kernel(place_ref, *refs):
        e_refs, rest = refs[:n_err], list(refs[n_err:])
        x, s, zp, m, v, fl = rest[:6]
        rest = rest[6:]
        if last:
            if out_prev is not None:
                rest = rest[1:]
            out, err, grad = rest
            streams = [v, fl]
        else:
            w, out, send, keep, err, grad, delta = rest
            streams = [v, fl, w]
        if len(errs) == 1:
            (err,) = e_refs
        else:
            base = 0
            for ref, at in zip(e_refs, starts):
                err[base:base + ref.shape[0], :] = ref[:, at:at + cols]
                base += ref.shape[0]

        def tile(*tiles):
            v_t, fl_t, out_t = tiles[0], tiles[1], tiles[-1]
            g = pl.program_id(0)
            features = pl.ds(pl.multiple_of(g * ROWS, ROWS), ROWS)
            scales, zero = steps_of(s[:, lanes]), None if last else zp[:, lanes].astype(f32)
            grad[...] = lax.dot_general(x[:, features], err[...], (((0,), (0,)), ((), ())), preferred_element_type=f32)

            def strip(start, i):
                at = pl.ds(start, STRIP)
                code = fl_t[at, :].astype(f32)
                old = v_t[at, :].astype(f32)
                mask = m[g * (ROWS // BLOCK) + i, :, lanes]
                new = update_rows(grad[at, :], jnp.tanh(0.5 * old), old, code, scales, mask)
                out_t[at, :] = new.astype(out_t.dtype)
                if not last:
                    to = pl.ds(pl.multiple_of(g * ROWS + start, STRIP), STRIP)
                    delta[to, :] = delta_rows(jnp.tanh(0.5 * new), code, tiles[2][at, :].astype(f32), scales, zero, mask)

            by_rows(ROWS, strip)

        def spec(c):
            return pl.BlockSpec((ROWS, cols), lambda g: (g, c))

        pltpu.emit_pipeline(
            tile, grid=(d // ROWS,),
            in_specs=[spec(v_col // cols), spec(code_col // cols)] + [spec(here)] * (len(streams) - 2),
            out_specs=[spec(here if last else 0)],
        )(*streams, out)

        if not last:
            def two(c, carry):
                part = jnp.dot(x[pl.ds(pl.multiple_of(c * 2 * rows, 16), 2 * rows), :], delta[...], preferred_element_type=f32)
                at = pl.multiple_of(c * rows, 16)
                split_rows(part[:rows, :], place_ref[0], send, keep, at, slice(None))
                split_rows(part[rows:, :], place_ref[0], send, keep, at + rows // 2, slice(None))
                return carry

            lax.fori_loop(0, 2, two, 0)

    operands = [place, *errs, x_full, scales, zeros, kept, rounding, codes]
    in_specs = [SMEM] + [VMEM] * (n_err + 4) + [HBM] * 2
    scratch = [pltpu.VMEM((tokens, cols), bf16), pltpu.VMEM((ROWS, cols), f32)]
    aliases = {}
    if last:
        if out_prev is not None:
            aliases = {len(operands): 0}
            operands.append(out_prev)
            in_specs.append(HBM)
        out_specs = [HBM]
        out_shape = [pltpu.HBM(weight.shape, f32)]
    else:
        operands.append(weight)
        in_specs.append(HBM)
        out_specs = [HBM, VMEM, VMEM]
        out_shape = [pltpu.HBM((d, cols), bf16)] + [jax.ShapeDtypeStruct((tokens // 2, cols), bf16)] * 2
        scratch.append(pltpu.VMEM((d, cols), bf16))
    return chain.call(
        kernel, "backward_last" if last else "backward_forward", operands, in_specs, out_specs, out_shape,
        (7.0 if last else 14.5) * cols / 512, scratch=scratch, aliases=aliases, late_hbm=last, mib=14 if last else 22,
    )


def swap_loop(a, core0, core1, n):
    pairs = [(i * n + j, (i ^ (core1 if j % 2 else core0)) * n + j) for i in range(4) for j in range(n)]
    return lax.ppermute(a, ("loop", "dp"), pairs)


def swap_core(a, n):
    return lax.ppermute(a, "dp", [(i, i ^ 1) for i in range(n)])


def spread(a, step, n):
    pairs = []
    for z in range(n // 2):
        if z - step >= 0 and z + 1 < n // 2:
            pairs.append((2 * z, 2 * z + 2))
        if z + step < n // 2 and z - 1 >= 0:
            pairs.append((2 * z + 1, 2 * z - 1))
    return lax.ppermute(a, "dp", pairs)


DELTAS = [512, 1280]
OWN = [512, 1280]
NEAR = [512, 1280]
MID = [512, 512, 768]
FAR = [512, 512, 768]
GROUPS = [512, 512, 512, 256]
ORDER = [
    "D0", "K0", "Fo0", "D1", "Po0", "Fo1", "Eo0", "G1", "K1", "Po1", "Fn0", "Fn1", "Ro0", "Eo1", "Pn0", "G2",
    "K2", "Pn1", "Fm0", "Fm1", "Ro1", "En0", "En1", "G3", "Fm2", "Rn0", "K3", "Ff0", "Pm0", "Pm1", "Ff1", "Pf0",
    "Rn1", "Em0", "Pf1", "Ff2", "Ef0", "Em1", "Ef1", "Pm2", "Rm0", "Pf2", "Rf0", "B0", "Em2", "Rf1", "Rm1", "Ef2",
    "B1", "Ps0", "Rm2", "Rf2", "B2", "Ps1", "Es0", "B3", "Ps2", "Es1", "Ps3", "Rs0", "L0", "Es2", "Rs1", "L1",
    "Es3", "Rs2", "L2", "Rs3", "L3",
]


def piped(tokens, weight, rounding, floor_codes, scale_codes, zero_codes, block_mask):
    n = 8
    rows = 2 * tokens.shape[0]
    scale = 2.0 / (tokens.shape[0] * n)
    width = weight.shape[1]
    loop_at, dp_at = lax.axis_index("loop"), lax.axis_index("dp")
    core, z = dp_at % 2, dp_at // 2
    place = jnp.stack([jnp.where(core == 0, loop_at % 2, loop_at // 2), z, core]).astype(jnp.int32)
    scales, zeros = scale_codes[None, :], zero_codes[None, :]
    weight, rounding, floor_codes = (pltpu.with_memory_space_constraint(a, pltpu.HBM) for a in (weight, rounding, floor_codes))
    kept = jnp.repeat(block_mask.astype(f32), BLOCK, axis=1)[:, None, :]
    chain = Chain()

    def ranges(widths):
        starts = [sum(widths[:i]) for i in range(len(widths))]
        return list(zip(starts, widths[:-1] + [width - starts[-1]]))

    blocks = ranges(DELTAS)
    parts = {"o": ranges(OWN), "n": ranges(NEAR), "m": ranges(MID), "f": ranges(FAR)}
    groups = ranges(GROUPS)
    other = swap_core(tokens, n)
    came, passed = {}, {}
    codes = {}
    chunk, deltas, sent, kept_part, pairs, errs, second, out = {}, {}, {}, {}, {}, {}, {}, [None]

    def above(step):
        return lambda core: step - 1 if core == 1 else 3 + step - 1

    def below(step):
        return lambda core: step - 1 if core == 0 else 3 + step - 1

    near_of = [above(1), above(1), below(1), below(1)]
    mid_of = [above(2), below(1), above(1), below(2)]
    far_of = [above(3), above(2), below(2), below(3)]

    def home(table, col):
        i = max(i for i, (start, _) in enumerate(table) if start <= col)
        return i, col - table[i][0]

    def pieces_of(col, cols):
        out = []
        for i, (start, count) in enumerate(blocks):
            low, high = max(start, col), min(start + count, col + cols)
            if low < high:
                out.append((deltas[i], low - start, high - low))
        return out

    for step in ORDER:
        kind, arg = step[0], step[1:]
        if kind == "K":
            if arg == "0":
                chunk["o"] = choose(chain, place, [tokens, other], [], [], "own")
                came[1] = spread(chunk["o"], 0, n)
            elif arg == "1":
                near = [lambda z, core: 0 if near_of[z](core) == 0 else 1]
                chunk["n"] = choose(chain, place, [], [came[1], passed[1]], near, "near")
            elif arg == "2":
                chunk["m"] = choose(chain, place, [], [came[1], came[2], passed[1], passed[2]],
                                    [lambda z, core: {0: 0, 1: 1, 3: 2, 4: 3}[mid_of[z](core)]], "mid")
            else:
                chunk["f"] = choose(chain, place, [chunk["o"], chunk["n"], chunk["m"]], [came[2], came[3], passed[2], passed[3]],
                                    [lambda z, core: {1: 0, 2: 1, 4: 2, 5: 3}[far_of[z](core)]], "all_tokens")
        elif kind == "G":
            i = int(arg)
            came[i] = gate(chain, came[i])
            passed[i] = swap_core(came[i], n)
            if i < 3:
                came[i + 1] = spread(came[i], i, n)
        elif kind == "D":
            i = int(arg)
            deltas[i], codes[i] = first_delta(chain, *blocks[i], weight, rounding, floor_codes, scales, zeros, kept)
        elif kind == "F":
            x, first = (chunk["f"], 3 * rows) if arg[0] == "f" else (chunk[arg[0]], 0)
            sent[arg], kept_part[arg] = forward(chain, place, x, first, rows, pieces_of(*parts[arg[0]][int(arg[1])]))
        elif kind == "P":
            pairs[arg] = add(chain, kept_part[arg], swap_loop(sent[arg], 1, 2, n))
        elif kind == "E":
            mine = add(chain, pairs[arg], swap_loop(pairs[arg], 2, 1, n), scale)
            errs[arg] = (mine, swap_loop(mine, 1, 2, n))
        elif kind == "R":
            errs[arg] = join(chain, place, *errs[arg], rows)
        elif kind == "B":
            col, cols = groups[int(arg)]
            i, inner = home(blocks, col)
            found = [(c, *home(parts[c], col)) for c in "onmf"]
            second[arg], sent["s" + arg], kept_part["s" + arg] = backward(
                chain, place, [errs["%s%d" % (c, k)] for c, k, _ in found], [at for _, _, at in found],
                chunk["f"], weight, rounding, col, codes[i], inner, scales, zeros, kept, col, cols, None, False)
        elif kind == "L":
            col, cols = groups[int(arg)]
            i, inner = home(blocks, col)
            (out[0],) = backward(
                chain, place, [errs["s" + arg]], [0],
                chunk["f"], weight, second[arg], 0, codes[i], inner, scales, zeros, kept, col, cols, out[0], True)
    return out[0]


def solution(mesh):
    placed = (
        P("dp", "loop"),
        P("loop", "dp"),
        P("loop", "dp"),
        P("loop", "dp"),
        P("dp"),
        P("dp"),
        P("loop", "dp"),
    )
    per_device = piped if (mesh.shape["loop"], mesh.shape["dp"]) == (4, 8) else plain
    return jax.shard_map(
        per_device, mesh=mesh, in_specs=placed, out_specs=P("loop", "dp"), check_vma=False
    )
```
